32 devices in a mesh: member: 2 (over y), wave: 4 (over z), lev: 2 (over x), fld: 2 (over core).
Axes of the slice: x: 2, y: 2, z: 4, core: 2. Of those that a mesh axis runs over, the one named last changes fastest.
Arguments:
- spectral: bfloat16 [2048, 2, 48, 1024], P(('member', 'wave'), None, ('lev', 'fld')), parts along dimension 0, may hold values from -0.1796875 to 0.1796875
- legendre: bfloat16 [1024, 64, 1024], P('wave'), may hold values from -0.1875 to 0.1875
- wave_order: int32 [1024], replicated, may hold values from 0 to 1023, as said below
Outputs:
- grid: bfloat16 [2, 24, 256, 4096], P(None, 'fld', ('member', 'wave'), 'lev'), parts along dimension 2
The draws below stay inside these ranges and needn't reach their ends.
There are 2 independent parts, one for each index of `member`. The reference program is written for one: setup_inputs(seed, part) draws one part's arguments, and reference() takes and returns one part's arrays. A program takes and returns all parts, laid end to end along the dimension named above; an argument that names none is the same for every part. Nothing has to cross between parts.
Inputs may be any that keep to these rules, and one draw needn't show every extreme that they name: `wave_order`: a permutation; each block of 256 slots (the slots of one index of wave) holds 128 wavenumbers m below 512 together with 1023 - m for each, in some order.
All inputs are finite; a program needn't handle non-finite values.
Results may differ from the reference program's by a relative error of at most 0.0055.
Values may be sent and summed in bfloat16 or wider, within the bound.
No kernel may reach another device: no remote copies, remote signals or barrier semaphores. Data moves between devices by JAX's collectives and lax.ppermute only.
A program may use at most 192 MiB of HBM per device.

```python
import math
import jax
import jax.numpy as jnp
from jax import lax

M = 1024
NLON = 4096
LATH = 64
LAT = 128
COLUMNS = 48
WAVES_DEV = 256
N_LEV = 2


def draw_wave_order(key, part):
    key = jax.random.fold_in(key, 11)
    first_key, second_key = jax.random.split(key)
    owners = M // WAVES_DEV
    lower = jax.random.permutation(first_key, M // 2).reshape(owners, WAVES_DEV // 2)
    blocks = jnp.concatenate([lower, M - 1 - lower], axis=1)
    inner_keys = jax.random.split(second_key, owners)
    inner = jax.vmap(lambda sub_key: jax.random.permutation(sub_key, WAVES_DEV))(inner_keys)
    order = jnp.take_along_axis(blocks, inner, axis=1)
    return order.reshape(M).astype(jnp.int32)


def shard_levels(stream_key, dims, cuts, smallest, top_value):
    def one(position, shards_of):
        heights = jax.random.uniform(jax.random.fold_in(jax.random.fold_in(stream_key, 6), position), (shards_of,), jnp.float32, smallest / len(cuts), top_value / len(cuts))
        return jnp.repeat(jnp.exp(heights), dims[position] // shards_of).reshape((-1,) + (1,) * (len(dims) - position - 1))

    gain = one(*cuts[0])
    for cut in cuts[1:]:
        gain = gain * one(*cut)
    return gain


def bell_draw(key, shape, deviation, limit, cuts=(), kind=jnp.bfloat16):
    values = jax.random.normal(key, shape, jnp.float32) * deviation
    if len(cuts) > 0:
        values = shard_levels(key, shape, cuts, -0.22, 0.18) * values
    return jnp.clip(values, min=-limit, max=limit).astype(kind)


def setup_inputs(seed: int = 0, part: int = 0) -> dict:
    splits = jax.random.split(jax.random.key(seed), 4)
    own_keys = jax.random.split(jax.random.fold_in(splits[3], part), 4)
    spectral = bell_draw(own_keys[0], (M, 2, COLUMNS, M), 0.03, 0.1796875, ((0, 4), (2, 4)))
    legendre = bell_draw(splits[1], (M, LATH, M), M ** -0.5, 0.1875, ((0, 4),))
    wave_order = draw_wave_order(jax.random.fold_in(splits[3], 71), part)
    return dict(spectral=spectral, legendre=legendre, wave_order=wave_order)


def longitude_sum(fourier, wave_order, lon_start, width):
    slots = fourier.shape[0]
    columns_here = fourier.shape[2]
    rows_here = fourier.shape[3]
    lon_index = lon_start + jnp.arange(width, dtype=jnp.int32)
    phases = (wave_order[:, None] * lon_index[None, :]) % NLON
    angles = phases.astype(jnp.float32) * (2.0 * math.pi / NLON)
    weights = jnp.where(wave_order == 0, 1.0, 2.0).astype(jnp.float32)[:, None]
    cosines = (weights * jnp.cos(angles)).astype(jnp.bfloat16)
    sines = (weights * jnp.sin(angles)).astype(jnp.bfloat16)
    table = jnp.concatenate([cosines, -sines], axis=0)
    left_side = fourier.transpose(2, 3, 1, 0).reshape(columns_here * rows_here, 2 * slots)
    values = jnp.dot(left_side, table, preferred_element_type=jnp.float32)
    return values.astype(jnp.bfloat16).reshape(columns_here, rows_here, width)


def reference(spectral, legendre, wave_order):
    degrees = jnp.arange(M, dtype=jnp.int32)

    def one_slot(inputs):
        table_rows, coeffs, wavenum = inputs
        keep = degrees >= wavenum
        coeffs = jnp.where(keep[None, None, :], coeffs, jnp.zeros((), coeffs.dtype))
        signs = (1 - 2 * ((degrees + wavenum) % 2)).astype(table_rows.dtype)
        mirrored = jnp.concatenate([table_rows, table_rows * signs[None, :]], axis=0)
        flat_coeffs = coeffs.reshape(2 * COLUMNS, M)
        result = jnp.dot(flat_coeffs, mirrored.T, preferred_element_type=jnp.float32)
        return result.reshape(2, COLUMNS, LAT)

    fourier = lax.map(one_slot, (legendre, spectral, wave_order)).astype(jnp.bfloat16)
    values = longitude_sum(fourier, wave_order, jnp.int32(0), NLON)
    return values.reshape(N_LEV, COLUMNS // N_LEV, LAT, NLON)
```

```python
import functools
import math

import jax
import jax.numpy as jnp
from jax import lax
from jax.experimental import pallas as pl
from jax.experimental.pallas import tpu as pltpu
from jax.sharding import PartitionSpec as P

NLON = 4096
GROUP = 64
STEP = 16
MIB = 1 << 20


def slot_columns(order_ref, first, count):
    rows = lax.broadcasted_iota(jnp.int32, (8, 128), 0)
    pieces = []
    for base in range(0, count, 8):
        piece = jnp.full((8, 128), order_ref[first + base], jnp.int32)
        for row in range(1, 8):
            piece = jnp.where(rows == row, order_ref[first + base + row], piece)
        pieces.append(piece)
    return jnp.concatenate(pieces, axis=0)


def legendre_kernel(cuts, first_slot, order_ref, spectral_ref, legendre_ref, *rest):
    waves = lax.axis_size("wave")
    out_refs, (by_slot, turned) = rest[:-2], rest[-2:]
    columns = spectral_ref.shape[1]
    degrees = spectral_ref.shape[3]
    rows = legendre_ref.shape[1]
    mine = lax.axis_index("wave")
    slots_here = order_ref.shape[0] // waves
    group, inner = pl.program_id(0), pl.program_id(1)
    slot = mine * slots_here + first_slot + group * GROUP + inner * STEP
    wavenums = slot_columns(order_ref, slot, STEP)
    lanes = lax.broadcasted_iota(jnp.int32, (STEP, 128), 1)
    keep, signed = [], []
    for start in range(0, degrees, 128):
        degree = lanes + start
        kept = jnp.where(degree >= wavenums, 1.0, 0.0)
        keep.append(kept.astype(jnp.bfloat16))
        odd = (degree + wavenums) & 1
        signed.append(jnp.where(odd == 1, -kept, kept).astype(jnp.bfloat16))
    keep = jnp.concatenate(keep, axis=1)
    signed = jnp.concatenate(signed, axis=1)
    for s in range(STEP):
        coeffs = spectral_ref[s].reshape(2 * columns, degrees)
        both = jnp.concatenate([coeffs * keep[s : s + 1], coeffs * signed[s : s + 1]], axis=0)
        by_slot[:, inner * STEP + s, :] = lax.dot_general(
            both, legendre_ref[s], (((1,), (1,)), ((), ())), preferred_element_type=jnp.float32
        )

    @pl.when(inner == GROUP // STEP - 1)
    def _():
        for pair in range(2 * columns):
            turned[pair] = jnp.concatenate([by_slot[2 * pair].T, by_slot[2 * pair + 1].T], axis=1)
        rows_dest = 2 * rows // waves
        half = waves // 2
        index = 0
        for shift in range(waves):
            dest = lax.rem(mine + shift, waves)
            side, block = dest // half, lax.rem(dest, half)
            for start, stop in cuts:
                piece = turned[
                    pl.ds(side * columns + start, stop - start),
                    pl.ds(pl.multiple_of(block * rows_dest, rows_dest), rows_dest),
                    :,
                ]
                flat = piece.reshape((stop - start) * rows_dest, 2 * GROUP)
                out_refs[index][0] = flat.astype(jnp.bfloat16)
                index += 1


def legendre_part(spectral, legendre, wave_order, first_group, groups, cuts):
    waves = lax.axis_size("wave")
    slots, columns, parts, degrees = spectral.shape
    rows = legendre.shape[1]
    rows_dest = 2 * rows // waves
    steps = GROUP // STEP
    first_step = first_group * steps
    shapes = [
        jax.ShapeDtypeStruct((groups, (stop - start) * rows_dest, 2 * GROUP), jnp.bfloat16)
        for _ in range(waves)
        for start, stop in cuts
    ]
    outs = pl.pallas_call(
        functools.partial(legendre_kernel, cuts, first_group * GROUP),
        grid_spec=pltpu.PrefetchScalarGridSpec(
            num_scalar_prefetch=1,
            grid=(groups, steps),
            in_specs=[
                pl.BlockSpec((STEP, columns, parts, degrees), lambda g, i, o: (first_step + g * steps + i, 0, 0, 0)),
                pl.BlockSpec((STEP, rows, degrees), lambda g, i, o: (first_step + g * steps + i, 0, 0)),
            ],
            out_specs=[pl.BlockSpec((1,) + s.shape[1:], lambda g, i, o: (g, 0, 0)) for s in shapes],
            scratch_shapes=[
                pltpu.VMEM((4 * columns, GROUP, rows), jnp.float32),
                pltpu.VMEM((2 * columns, rows, 2 * GROUP), jnp.float32),
            ],
        ),
        out_shape=shapes,
        compiler_params=pltpu.CompilerParams(vmem_limit_bytes=40 * MIB),
        cost_estimate=pl.CostEstimate(
            flops=groups * GROUP * 8 * columns * rows * degrees,
            bytes_accessed=groups * GROUP * degrees * 2 * (2 * columns + rows),
            transcendentals=0,
        ),
    )(wave_order, spectral, legendre)
    return [outs[k * len(cuts) : (k + 1) * len(cuts)] for k in range(waves)]


def cos_sin(phase):
    quarter = NLON // 4
    quadrant = (phase + quarter // 2) // quarter
    x = (phase - quadrant * quarter).astype(jnp.float32) * (2.0 * math.pi / NLON)
    y = x * x
    sine = x * (1.0 + y * (-1.0 / 6 + y * (1.0 / 120 + y * (-1.0 / 5040 + y * (1.0 / 362880)))))
    cosine = 1.0 + y * (-0.5 + y * (1.0 / 24 + y * (-1.0 / 720 + y * (1.0 / 40320 + y * (-1.0 / 3628800)))))
    swap = (quadrant & 1) == 1
    c = jnp.where(swap, sine, cosine)
    s = jnp.where(swap, cosine, sine)
    c = jnp.where(((quadrant + 1) & 2) == 2, -c, c)
    s = jnp.where((quadrant & 2) == 2, -s, s)
    return c, s


def table_kernel(order_ref, out_ref):
    waves = lax.axis_size("wave")
    slots_here = order_ref.shape[0] // waves
    groups = slots_here // GROUP
    shift, group = pl.program_id(0) // groups, pl.program_id(0) % groups
    source = lax.rem(lax.axis_index("wave") + waves - shift, waves)
    width = out_ref.shape[2]
    lon_start = lax.axis_index("lev") * width
    wavenums = slot_columns(order_ref, source * slots_here + group * GROUP, GROUP)
    lanes = lax.broadcasted_iota(jnp.int32, (GROUP, 128), 1)
    fine_cos, fine_sin = cos_sin((wavenums * lanes) & (NLON - 1))
    coarse_cos, coarse_sin = cos_sin((wavenums * (lon_start + 128 * lanes)) & (NLON - 1))
    weight = jnp.where(wavenums == 0, 1.0, 2.0)
    coarse_cos, coarse_sin = coarse_cos * weight, coarse_sin * weight
    for box in range(width // 128):
        c, s = coarse_cos[:, box : box + 1], coarse_sin[:, box : box + 1]
        cosines = c * fine_cos - s * fine_sin
        sines = s * fine_cos + c * fine_sin
        out_ref[0, 0:GROUP, box * 128 : (box + 1) * 128] = cosines.astype(jnp.bfloat16)
        out_ref[0, GROUP : 2 * GROUP, box * 128 : (box + 1) * 128] = (-sines).astype(jnp.bfloat16)


def longitude_table(wave_order):
    blocks = wave_order.shape[0] // GROUP
    width = NLON // lax.axis_size("lev")
    table = pl.pallas_call(
        table_kernel,
        grid_spec=pltpu.PrefetchScalarGridSpec(
            num_scalar_prefetch=1,
            grid=(blocks,),
            in_specs=[],
            out_specs=pl.BlockSpec((1, 2 * GROUP, width), lambda i, o: (i, 0, 0)),
        ),
        out_shape=jax.ShapeDtypeStruct((blocks, 2 * GROUP, width), jnp.bfloat16),
        compiler_params=pltpu.CompilerParams(vmem_limit_bytes=16 * MIB),
        cost_estimate=pl.CostEstimate(
            flops=blocks * GROUP * width * 20, bytes_accessed=blocks * 4 * GROUP * width, transcendentals=0
        ),
    )(wave_order)
    return table.reshape(blocks * 2 * GROUP, width)


def longitude_kernel(layout, n_in, *refs):
    in_refs, table_ref = refs[:n_in], refs[n_in]
    out_ref, left = refs[-2], refs[-1]
    levs = lax.axis_size("lev")
    height = left.shape[0] // levs

    @pl.when(pl.program_id(0) == 0)
    def _():
        for shift, blocks in enumerate(layout):
            for place, (operand, group) in enumerate(blocks):
                left[shift * height : (shift + 1) * height, place * 2 * GROUP : (place + 1) * 2 * GROUP] = in_refs[
                    operand
                ][group]

    values = jnp.dot(left[...], table_ref[...], preferred_element_type=jnp.float32)
    for shift in range(levs):
        lev = lax.rem(lax.axis_index("lev") + levs - shift, levs)
        part = values[shift * height : (shift + 1) * height]
        out_ref[lev] = part.reshape(out_ref.shape[1:]).astype(jnp.bfloat16)


def longitude_part(early, late, table, grid, cut, columns, rows_dest):
    levs = lax.axis_size("lev")
    start, stop = cut
    count = stop - start
    depth, width = table.shape
    tile = min(512, width)
    operands, specs, layout = [], [], []
    for lev_shift in range(levs):
        blocks = []
        for wave_shift in range(len(early[lev_shift])):
            first = early[lev_shift][wave_shift]
            blocks += [(len(operands), g) for g in range(first.shape[0])]
            operands.append(first)
            specs.append(
                pl.BlockSpec((first.shape[0], count * rows_dest, 2 * GROUP), lambda j, b=start // count: (0, b, 0))
            )
            if late is not None:
                second = late[lev_shift][wave_shift]
                blocks += [(len(operands), g) for g in range(second.shape[0])]
                operands.append(second)
                specs.append(pl.BlockSpec(second.shape, lambda j: (0, 0, 0)))
        layout.append(blocks)
    n_in = len(operands)
    operands.append(table)
    specs.append(pl.BlockSpec((depth, tile), lambda j: (0, j)))
    aliases = {}
    if grid is not None:
        aliases = {len(operands): 0}
        operands.append(grid)
        specs.append(pl.BlockSpec(memory_space=pl.ANY))
    out_block = (levs, count, rows_dest, tile)
    return pl.pallas_call(
        functools.partial(longitude_kernel, layout, n_in),
        grid=(width // tile,),
        in_specs=specs,
        out_specs=pl.BlockSpec(out_block, lambda j, b=start // count: (0, b, 0, j)),
        out_shape=jax.ShapeDtypeStruct((levs, columns, rows_dest, width), jnp.bfloat16),
        scratch_shapes=[pltpu.VMEM((levs * count * rows_dest, depth), jnp.bfloat16)],
        input_output_aliases=aliases,
        compiler_params=pltpu.CompilerParams(vmem_limit_bytes=40 * MIB),
        cost_estimate=pl.CostEstimate(
            flops=2 * levs * count * rows_dest * depth * width,
            bytes_accessed=2 * (depth * width + levs * count * rows_dest * (depth + width)),
            transcendentals=0,
        ),
    )(*operands)


def send(array, axis, shift):
    size = lax.axis_size(axis)
    return lax.ppermute(array, axis, [(i, (i + shift) % size) for i in range(size)])


def spread(pieces):
    own = [pieces[0]] + [send(pieces[shift], "wave", shift) for shift in range(1, len(pieces))]
    levs = lax.axis_size("lev")
    return [own] + [[send(piece, "lev", shift) for piece in own] for shift in range(1, levs)]


def shards(spectral, legendre, wave_order):
    slots, _, columns, _ = spectral.shape
    waves = lax.axis_size("wave")
    rows_dest = 2 * legendre.shape[1] // waves
    groups = slots // GROUP
    cuts = [(0, 4), (4, 8), (8, 12)] if columns == 12 else [(0, columns)]
    spectral = spectral.transpose(0, 2, 1, 3)
    first = legendre_part(spectral, legendre, wave_order, 0, 1, [(0, columns)])
    early = spread([pieces[0] for pieces in first])
    lates = [None] * len(cuts)
    if groups > 1:
        second = legendre_part(spectral, legendre, wave_order, 1, groups - 1, cuts)
        lates = [spread([pieces[i] for pieces in second]) for i in range(len(cuts))]
    table = longitude_table(wave_order)
    grid = None
    for cut, late in zip(cuts, lates):
        grid = longitude_part(early, late, table, grid, cut, columns, rows_dest)
    return grid


def solution(mesh):
    in_specs = (P(("member", "wave"), None, ("lev", "fld"), None), P("wave", None, None), P())
    out_specs = P(None, "fld", ("member", "wave"), "lev")
    return jax.shard_map(shards, mesh=mesh, in_specs=in_specs, out_specs=out_specs, check_vma=False)
```

```python
import functools
import math

import jax
import jax.numpy as jnp
import numpy as np
from jax import lax
from jax.experimental import pallas as pl
from jax.experimental.pallas import tpu as pltpu
from jax.sharding import PartitionSpec as P

NLON = 4096
PAIRS = 32
GROUP = 2 * PAIRS
STEP = 16
CHUNKS = (2, 2)
MIB = 1 << 20


def pair_lists(wave_order, waves):
    blocks = wave_order.reshape(waves, -1)
    slots = blocks.shape[1]
    rank = jnp.sum((blocks[:, None, :] < blocks[:, :, None]).astype(jnp.int32), axis=2)
    places = jnp.arange(slots, dtype=jnp.int32)
    hit = rank[:, None, :] == places[None, :, None]
    order = jnp.sum(jnp.where(hit, places[None, None, :], 0), axis=2)
    lower = jnp.sum(jnp.where(hit[:, : slots // 2], blocks[:, None, :], 0), axis=2)
    return order.reshape(-1), lower.reshape(-1)


def rows_of(values_ref, first, count):
    rows = lax.broadcasted_iota(jnp.int32, (8, 128), 0)
    pieces = []
    for base in range(0, count, 8):
        piece = jnp.full((8, 128), values_ref[first + base], jnp.int32)
        for row in range(1, 8):
            piece = jnp.where(rows == row, values_ref[first + base + row], piece)
        pieces.append(piece)
    return jnp.concatenate(pieces, axis=0)


def legendre_kernel(first_group, groups, order_ref, lower_ref, spectral_ref, legendre_ref, *rest):
    waves = lax.axis_size("wave")
    out_refs = rest[:waves]
    coeffs_ref, values_ref, by_slot, turned, sems = rest[waves:]
    columns, tiles = spectral_ref.shape[1], spectral_ref.shape[2]
    rows = 8 * legendre_ref.shape[1]
    mine = lax.axis_index("wave")
    slots_here = spectral_ref.shape[0]
    group = pl.program_id(0)
    steps = PAIRS // STEP

    @pl.when(group == 0)
    def _():
        @pl.loop(0, groups * PAIRS)
        def _(p):
            rank = first_group * PAIRS + p
            low = order_ref[mine * slots_here + rank]
            high = order_ref[mine * slots_here + slots_here - 1 - rank]
            t = lower_ref[mine * (slots_here // 2) + rank] // 128
            for kind, (source, target) in enumerate(((legendre_ref, values_ref), (spectral_ref, coeffs_ref))):
                sem = sems.at[kind, p // STEP]
                pltpu.make_async_copy(
                    source.at[low, :, pl.ds(t, tiles - t)], target.at[p, :, pl.ds(0, tiles - t)], sem
                ).start()
                pltpu.make_async_copy(
                    source.at[high, :, pl.ds(tiles - 1 - t, t + 1)], target.at[p, :, pl.ds(tiles - t, t + 1)], sem
                ).start()

    lanes = lax.broadcasted_iota(jnp.int32, (STEP, 128), 1)

    @pl.loop(0, steps)
    def _(step):
        place = group * steps + step
        first = place * STEP
        wavenums = rows_of(lower_ref, mine * (slots_here // 2) + first_group * PAIRS + first, STEP)
        for kind, target in enumerate((values_ref, coeffs_ref)):
            arrived = target.at[pl.ds(first, STEP)]
            pltpu.make_async_copy(arrived, arrived, sems.at[kind, place]).wait()
        t, inside = wavenums // 128, wavenums & 127
        parity = jnp.where(((lanes + wavenums) & 1) == 1, -1.0, 1.0)
        masks = [[], [], [], []]
        for i in range(tiles + 1):
            low = t + i < tiles
            if i == 0:
                low = lanes >= inside
            high = (t + i > tiles) | ((t + i == tiles) & (lanes >= 127 - inside))
            low, high = jnp.where(low, 1.0, 0.0), jnp.where(high, 1.0, 0.0)
            for mask, value in zip(masks, (low, low * parity, high, -high * parity)):
                mask.append(value.astype(jnp.bfloat16))
        masks = [jnp.concatenate(mask, axis=1) for mask in masks]
        for s in range(STEP):
            coeffs = jnp.concatenate(
                [coeffs_ref[first + s, :, i].reshape(2 * columns, 128) for i in range(tiles + 1)], axis=1
            )
            values = jnp.concatenate([values_ref[first + s, :, i].reshape(rows, 128) for i in range(tiles + 1)], axis=1)
            left = jnp.concatenate([coeffs * mask[s : s + 1] for mask in masks], axis=0)
            sums = lax.dot_general(left, values, (((1,), (1,)), ((), ())), preferred_element_type=jnp.float32)
            by_slot[:, step * STEP + s, :] = sums[: 4 * columns]
            by_slot[:, PAIRS + step * STEP + s, :] = sums[4 * columns :]

    for pair in range(2 * columns):
        turned[pair] = jnp.concatenate([by_slot[2 * pair].T, by_slot[2 * pair + 1].T], axis=1)
    rows_dest = 2 * rows // waves
    half = waves // 2
    for shift in range(waves):
        dest = lax.rem(mine + shift, waves)
        side, block = dest // half, lax.rem(dest, half)
        piece = turned[
            pl.ds(side * columns, columns), pl.ds(pl.multiple_of(block * rows_dest, rows_dest), rows_dest), :
        ]
        out_refs[shift][0] = piece.reshape(columns * rows_dest, 2 * GROUP).astype(jnp.bfloat16)


def legendre_part(spectral, legendre, lists, first_group, groups):
    waves = lax.axis_size("wave")
    slots, columns, tiles = spectral.shape[:3]
    rows = 8 * legendre.shape[1]
    rows_dest = 2 * rows // waves
    pairs = groups * PAIRS
    shape = jax.ShapeDtypeStruct((groups, columns * rows_dest, 2 * GROUP), jnp.bfloat16)
    return pl.pallas_call(
        functools.partial(legendre_kernel, first_group, groups),
        grid_spec=pltpu.PrefetchScalarGridSpec(
            num_scalar_prefetch=2,
            grid=(groups,),
            in_specs=[pl.BlockSpec(memory_space=pl.ANY)] * 2,
            out_specs=[pl.BlockSpec((1,) + shape.shape[1:], lambda g, *_: (g, 0, 0))] * waves,
            scratch_shapes=[
                pltpu.VMEM((pairs, columns, tiles + 1, 2, 128), jnp.bfloat16),
                pltpu.VMEM((pairs, rows // 8, tiles + 1, 8, 128), jnp.bfloat16),
                pltpu.VMEM((4 * columns, GROUP, rows), jnp.float32),
                pltpu.VMEM((2 * columns, rows, 2 * GROUP), jnp.float32),
                pltpu.SemaphoreType.DMA((2, pairs // STEP)),
            ],
        ),
        out_shape=[shape] * waves,
        compiler_params=pltpu.CompilerParams(vmem_limit_bytes=56 * MIB),
        cost_estimate=pl.CostEstimate(flops=1 << 10, bytes_accessed=1 << 10, transcendentals=0),
    )(*lists, spectral, legendre)


def cos_sin(phase):
    quarter = NLON // 4
    quadrant = (phase + quarter // 2) // quarter
    x = (phase - quadrant * quarter).astype(jnp.float32) * (2.0 * math.pi / NLON)
    y = x * x
    sine = x * (1.0 + y * (-1.0 / 6 + y * (1.0 / 120 + y * (-1.0 / 5040 + y * (1.0 / 362880)))))
    cosine = 1.0 + y * (-0.5 + y * (1.0 / 24 + y * (-1.0 / 720 + y * (1.0 / 40320 + y * (-1.0 / 3628800)))))
    swap = (quadrant & 1) == 1
    c = jnp.where(swap, sine, cosine)
    s = jnp.where(swap, cosine, sine)
    c = jnp.where(((quadrant + 1) & 2) == 2, -c, c)
    s = jnp.where((quadrant & 2) == 2, -s, s)
    return c, s


def table_kernel(shifts_ref, groups_ref, lower_ref, out_ref):
    waves = lax.axis_size("wave")
    pairs_here = lower_ref.shape[0] // waves
    shift, group = shifts_ref[pl.program_id(0)], groups_ref[pl.program_id(0)]
    source = lax.rem(lax.axis_index("wave") + waves - shift, waves)
    width = out_ref.shape[1]
    lon_start = lax.axis_index("lev") * width
    lower = rows_of(lower_ref, source * pairs_here + group * PAIRS, PAIRS)
    wavenums = jnp.concatenate([lower, 2 * lower_ref.shape[0] - 1 - lower], axis=0)
    lanes = lax.broadcasted_iota(jnp.int32, (GROUP, 128), 1)
    fine_cos, fine_sin = cos_sin((wavenums * lanes) & (NLON - 1))
    coarse_cos, coarse_sin = cos_sin((wavenums * (lon_start + 128 * lanes)) & (NLON - 1))
    weight = jnp.where(wavenums == 0, 1.0, 2.0)
    coarse_cos, coarse_sin = coarse_cos * weight, coarse_sin * weight
    for box in range(width // 128):
        c, s = coarse_cos[:, box : box + 1], coarse_sin[:, box : box + 1]
        cosines = c * fine_cos - s * fine_sin
        sines = s * fine_cos + c * fine_sin
        out_ref[0:GROUP, box * 128 : (box + 1) * 128] = cosines.astype(jnp.bfloat16)
        out_ref[GROUP : 2 * GROUP, box * 128 : (box + 1) * 128] = (-sines).astype(jnp.bfloat16)


def longitude_table(lower, blocks):
    width = NLON // lax.axis_size("lev")
    shifts, groups = np.array(blocks, np.int32).T
    return pl.pallas_call(
        table_kernel,
        grid_spec=pltpu.PrefetchScalarGridSpec(
            num_scalar_prefetch=3,
            grid=(len(blocks),),
            in_specs=[],
            out_specs=pl.BlockSpec((2 * GROUP, width), lambda i, *_: (i, 0)),
        ),
        out_shape=jax.ShapeDtypeStruct((len(blocks) * 2 * GROUP, width), jnp.bfloat16),
        compiler_params=pltpu.CompilerParams(vmem_limit_bytes=16 * MIB),
        cost_estimate=pl.CostEstimate(flops=1 << 10, bytes_accessed=1 << 10, transcendentals=0),
    )(jnp.asarray(shifts), jnp.asarray(groups), lower)


def longitude_kernel(layout, n_in, last, *refs):
    in_refs, table_ref, rest = refs[:n_in], refs[n_in], refs[n_in + 1 :]
    out_ref, left = rest[-2:]
    levs = lax.axis_size("lev")
    height = left.shape[0] // levs

    @pl.when(pl.program_id(0) == 0)
    def _():
        for shift, blocks in enumerate(layout):
            for place, (operand, group) in enumerate(blocks):
                left[shift * height : (shift + 1) * height, place * 2 * GROUP : (place + 1) * 2 * GROUP] = in_refs[
                    operand
                ][group]

    for shift in range(levs):
        here = slice(shift * height, (shift + 1) * height)
        values = jnp.dot(left[here], table_ref[...], preferred_element_type=jnp.float32)
        if len(rest) == 3:
            values = values + rest[0][here]
        if last:
            lev = lax.rem(lax.axis_index("lev") + levs - shift, levs)
            out_ref[lev] = values.reshape(out_ref.shape[1:]).astype(jnp.bfloat16)
        else:
            out_ref[here] = values


def longitude_part(pieces, table, total, last, columns):
    levs = len(pieces)
    height = pieces[0][0].shape[1]
    depth, width = table.shape
    tile = min(512, width)
    operands, layout = [], []
    for row in pieces:
        blocks = []
        for piece in row:
            blocks += [(len(operands), g) for g in range(piece.shape[0])]
            operands.append(piece)
        layout.append(blocks)
    n_in = len(operands)
    specs = [pl.BlockSpec(piece.shape, lambda j: (0, 0, 0)) for piece in operands]
    operands.append(table)
    specs.append(pl.BlockSpec((depth, tile), lambda j: (0, j)))
    if total is not None:
        operands.append(total)
        specs.append(pl.BlockSpec((levs * height, tile), lambda j: (0, j)))
    if last:
        out_spec = pl.BlockSpec((levs, columns, height // columns, tile), lambda j: (0, 0, 0, j))
        out_shape = jax.ShapeDtypeStruct((levs, columns, height // columns, width), jnp.bfloat16)
    else:
        out_spec = pl.BlockSpec((levs * height, tile), lambda j: (0, j))
        out_shape = jax.ShapeDtypeStruct((levs * height, width), jnp.float32)
    return pl.pallas_call(
        functools.partial(longitude_kernel, layout, n_in, last),
        grid=(width // tile,),
        in_specs=specs,
        out_specs=out_spec,
        out_shape=out_shape,
        scratch_shapes=[pltpu.VMEM((levs * height, depth), jnp.bfloat16)],
        compiler_params=pltpu.CompilerParams(vmem_limit_bytes=32 * MIB),
        cost_estimate=pl.CostEstimate(flops=1 << 10, bytes_accessed=1 << 10, transcendentals=0),
    )(*operands)


def send(array, axis, shift):
    size = lax.axis_size(axis)
    return lax.ppermute(array, axis, [(i, (i + shift) % size) for i in range(size)])


def shards(spectral, legendre, wave_order):
    slots, parts, columns, degrees = spectral.shape
    waves, levs = lax.axis_size("wave"), lax.axis_size("lev")
    rows, tiles = legendre.shape[1], degrees // 128
    groups = slots // GROUP
    spectral = spectral.reshape(slots, parts, columns, tiles, 128).transpose(0, 2, 3, 1, 4)
    legendre = legendre.reshape(slots, rows // 8, 8, tiles, 128).transpose(0, 1, 3, 2, 4)
    order, lower = pair_lists(wave_order, waves)
    sizes = list(CHUNKS) if groups == sum(CHUNKS) else [groups]
    far_first = sorted(range(1, waves), key=lambda shift: (abs(2 * shift - waves), shift))
    blocks, arrived = {}, {}
    first_group = 0
    lists = (order, lower)
    for chunk, size in enumerate(sizes):
        outs = legendre_part(spectral, legendre, lists, first_group, size)
        lists = lax.optimization_barrier((order, lower, outs[0]))[:2]
        for shift in [0] + far_first:
            piece = outs[shift]
            if shift != 0:
                if chunk > 0:
                    before = (chunk - 1, shift)
                    piece, arrived[before] = lax.optimization_barrier((piece, arrived[before]))
                piece = send(piece, "wave", shift)
            arrived[chunk, shift] = piece
            blocks[chunk, shift] = [(shift, first_group + g) for g in range(size)]
        first_group += size
    keys = list(arrived)
    late = far_first if len(sizes) > 1 else []
    cut = [[key for key in keys if key[0] < len(sizes) - 1 or key[1] not in late]]
    if late:
        cut.append([(len(sizes) - 1, shift) for shift in late])
    pieces = {}

    def relay(key):
        before = (key[0] - 1, key[1])
        piece = arrived[key]
        if before in pieces:
            tied = lax.optimization_barrier((piece, *pieces[before]))
            piece, pieces[before] = tied[0], list(tied[1:])
        pieces[key] = [piece] + [send(piece, "lev", lev) for lev in range(1, levs)]

    final = [key for key in keys if key[0] == len(sizes) - 1 and key[1] != 0]
    for key in keys:
        if key not in final:
            relay(key)
    if len(sizes) > 1:
        first_relayed = (len(sizes) - 2, far_first[0])
        tied = lax.optimization_barrier((lists[1], *pieces[first_relayed]))
        lists, pieces[first_relayed] = (order, tied[0]), list(tied[1:])
    tables = [longitude_table(lists[1], [block for name in names for block in blocks[name]]) for names in cut]
    for key in final:
        tied = lax.optimization_barrier((arrived[key], *tables))
        arrived[key], tables = tied[0], list(tied[1:])
        relay(key)
    total = None
    for index, names in enumerate(cut):
        rows_of_pieces = [[pieces[name][lev] for name in names] for lev in range(levs)]
        total = longitude_part(rows_of_pieces, tables[index], total, index == len(cut) - 1, columns)
    return total


def solution(mesh):
    in_specs = (P(("member", "wave"), None, ("lev", "fld"), None), P("wave", None, None), P())
    out_specs = P(None, "fld", ("member", "wave"), "lev")
    return jax.shard_map(shards, mesh=mesh, in_specs=in_specs, out_specs=out_specs, check_vma=False)
```

```python
import functools
import math

import jax
import jax.numpy as jnp
import numpy as np
from jax import lax
from jax.experimental import pallas as pl
from jax.experimental.pallas import tpu as pltpu
from jax.sharding import PartitionSpec as P

NLON = 4096
PAIRS = 32
GROUP = 2 * PAIRS
STEP = 16
CHUNKS = (2, 2)
MIB = 1 << 20


def pair_lists(wave_order, waves):
    blocks = wave_order.reshape(waves, -1)
    slots = blocks.shape[1]
    rank = jnp.sum((blocks[:, None, :] < blocks[:, :, None]).astype(jnp.int32), axis=2)
    places = jnp.arange(slots, dtype=jnp.int32)
    hit = rank[:, None, :] == places[None, :, None]
    order = jnp.sum(jnp.where(hit, places[None, None, :], 0), axis=2)
    lower = jnp.sum(jnp.where(hit[:, : slots // 2], blocks[:, None, :], 0), axis=2)
    return order.reshape(-1), lower.reshape(-1)


def rows_of(values_ref, first, count):
    rows = lax.broadcasted_iota(jnp.int32, (8, 128), 0)
    pieces = []
    for base in range(0, count, 8):
        piece = jnp.full((8, 128), values_ref[first + base], jnp.int32)
        for row in range(1, 8):
            piece = jnp.where(rows == row, values_ref[first + base + row], piece)
        pieces.append(piece)
    return jnp.concatenate(pieces, axis=0)


def legendre_kernel(first_group, groups, order_ref, lower_ref, spectral_ref, legendre_ref, *rest):
    waves = lax.axis_size("wave")
    out_refs = rest[:waves]
    coeffs_ref, values_ref, by_slot, turned, sems = rest[waves:]
    columns, tiles = spectral_ref.shape[1], spectral_ref.shape[2]
    rows = 8 * legendre_ref.shape[1]
    mine = lax.axis_index("wave")
    slots_here = spectral_ref.shape[0]
    group = pl.program_id(0)
    steps = PAIRS // STEP

    @pl.when(group == 0)
    def _():
        @pl.loop(0, groups * PAIRS, unroll=4)
        def _(p):
            rank = first_group * PAIRS + p
            low = order_ref[mine * slots_here + rank]
            high = order_ref[mine * slots_here + slots_here - 1 - rank]
            t = lower_ref[mine * (slots_here // 2) + rank] // 128
            for kind, (source, target) in enumerate(((legendre_ref, values_ref), (spectral_ref, coeffs_ref))):
                sem = sems.at[kind, p // STEP]
                pltpu.make_async_copy(
                    source.at[low, :, pl.ds(t, tiles - t)], target.at[p, :, pl.ds(0, tiles - t)], sem
                ).start()
                pltpu.make_async_copy(
                    source.at[high, :, pl.ds(tiles - 1 - t, t + 1)], target.at[p, :, pl.ds(tiles - t, t + 1)], sem
                ).start()

    lanes = lax.broadcasted_iota(jnp.int32, (STEP, 128), 1)

    @pl.loop(0, steps)
    def _(step):
        place = group * steps + step
        first = place * STEP
        wavenums = rows_of(lower_ref, mine * (slots_here // 2) + first_group * PAIRS + first, STEP)
        for kind, target in enumerate((values_ref, coeffs_ref)):
            arrived = target.at[pl.ds(first, STEP)]
            pltpu.make_async_copy(arrived, arrived, sems.at[kind, place]).wait()
        t, inside = wavenums // 128, wavenums & 127
        parity = jnp.where(((lanes + wavenums) & 1) == 1, -1.0, 1.0)
        always = tiles // 2 + 1
        low_keep, low_sign, high_keep, high_sign = [], [], [], []
        for i in range(tiles + 1):
            if i == 0:
                low = jnp.where(lanes >= inside, 1.0, 0.0)
            else:
                low = jnp.where(t + i < tiles, 1.0, 0.0)
            high = jnp.where((t + i > tiles) | ((t + i == tiles) & (lanes >= 127 - inside)), 1.0, 0.0)
            if i < tiles:
                low_keep.append(low.astype(jnp.bfloat16))
                low_sign.append((low * parity).astype(jnp.bfloat16))
            if i >= always:
                high_keep.append(high.astype(jnp.bfloat16))
                high_sign.append((-high * parity).astype(jnp.bfloat16))
        low_keep, low_sign, high_keep, high_sign = [
            jnp.concatenate(mask, axis=1) for mask in (low_keep, low_sign, high_keep, high_sign)
        ]
        for s in range(STEP):
            row = slice(s, s + 1)
            coeffs = jnp.concatenate(
                [coeffs_ref[first + s, :, i].reshape(2 * columns, 128) for i in range(tiles + 1)], axis=1
            )
            values = jnp.concatenate([values_ref[first + s, :, i].reshape(rows, 128) for i in range(tiles + 1)], axis=1)
            for place, part, keep, sign in (
                (step * STEP + s, slice(0, tiles * 128), low_keep, low_sign),
                (PAIRS + step * STEP + s, slice(always * 128, (tiles + 1) * 128), high_keep, high_sign),
            ):
                left = jnp.concatenate([coeffs[:, part] * keep[row], coeffs[:, part] * sign[row]], axis=0)
                by_slot[:, place, :] = lax.dot_general(
                    left, values[:, part], (((1,), (1,)), ((), ())), preferred_element_type=jnp.float32
                )

    for pair in range(2 * columns):
        both = jnp.concatenate([by_slot[2 * pair], by_slot[2 * pair + 1]], axis=0)
        turned[pair] = both.astype(jnp.bfloat16).T.astype(turned.dtype)
    rows_dest = 2 * rows // waves
    half = waves // 2
    for shift in range(waves):
        dest = lax.rem(mine + shift, waves)
        side, block = dest // half, lax.rem(dest, half)
        piece = turned[
            pl.ds(side * columns, columns), pl.ds(pl.multiple_of(block * rows_dest, rows_dest), rows_dest), :
        ]
        out_refs[shift][0] = piece.reshape(columns * rows_dest, 2 * GROUP).astype(jnp.bfloat16)


def legendre_part(spectral, legendre, lists, first_group, groups):
    waves = lax.axis_size("wave")
    slots, columns, tiles = spectral.shape[:3]
    rows = 8 * legendre.shape[1]
    rows_dest = 2 * rows // waves
    pairs = groups * PAIRS
    shape = jax.ShapeDtypeStruct((groups, columns * rows_dest, 2 * GROUP), jnp.bfloat16)
    return pl.pallas_call(
        functools.partial(legendre_kernel, first_group, groups),
        grid_spec=pltpu.PrefetchScalarGridSpec(
            num_scalar_prefetch=2,
            grid=(groups,),
            in_specs=[pl.BlockSpec(memory_space=pl.ANY)] * 2,
            out_specs=[pl.BlockSpec((1,) + shape.shape[1:], lambda g, *_: (g, 0, 0))] * waves,
            scratch_shapes=[
                pltpu.VMEM((pairs, columns, tiles + 1, 2, 128), jnp.bfloat16),
                pltpu.VMEM((pairs, rows // 8, tiles + 1, 8, 128), jnp.bfloat16),
                pltpu.VMEM((4 * columns, GROUP, rows), jnp.float32),
                pltpu.VMEM((2 * columns, rows, 2 * GROUP), jnp.float32),
                pltpu.SemaphoreType.DMA((2, pairs // STEP)),
            ],
        ),
        out_shape=[shape] * waves,
        compiler_params=pltpu.CompilerParams(vmem_limit_bytes=56 * MIB),
        cost_estimate=pl.CostEstimate(flops=1 << 10, bytes_accessed=1 << 10, transcendentals=0),
    )(*lists, spectral, legendre)


def cos_sin(phase):
    quarter = NLON // 4
    quadrant = (phase + quarter // 2) // quarter
    x = (phase - quadrant * quarter).astype(jnp.float32) * (2.0 * math.pi / NLON)
    y = x * x
    sine = x * (1.0 + y * (-1.0 / 6 + y * (1.0 / 120 + y * (-1.0 / 5040 + y * (1.0 / 362880)))))
    cosine = 1.0 + y * (-0.5 + y * (1.0 / 24 + y * (-1.0 / 720 + y * (1.0 / 40320 + y * (-1.0 / 3628800)))))
    swap = (quadrant & 1) == 1
    c = jnp.where(swap, sine, cosine)
    s = jnp.where(swap, cosine, sine)
    c = jnp.where(((quadrant + 1) & 2) == 2, -c, c)
    s = jnp.where((quadrant & 2) == 2, -s, s)
    return c, s


def table_kernel(shifts_ref, groups_ref, lower_ref, out_ref):
    waves = lax.axis_size("wave")
    pairs_here = lower_ref.shape[0] // waves
    shift, group = shifts_ref[pl.program_id(0)], groups_ref[pl.program_id(0)]
    source = lax.rem(lax.axis_index("wave") + waves - shift, waves)
    width = out_ref.shape[1]
    lon_start = lax.axis_index("lev") * width
    lower = rows_of(lower_ref, source * pairs_here + group * PAIRS, PAIRS)
    wavenums = jnp.concatenate([lower, 2 * lower_ref.shape[0] - 1 - lower], axis=0)
    lanes = lax.broadcasted_iota(jnp.int32, (GROUP, 128), 1)
    fine_cos, fine_sin = cos_sin((wavenums * lanes) & (NLON - 1))
    coarse_cos, coarse_sin = cos_sin((wavenums * (lon_start + 128 * lanes)) & (NLON - 1))
    weight = jnp.where(wavenums == 0, 1.0, 2.0)
    coarse_cos, coarse_sin = coarse_cos * weight, coarse_sin * weight
    for box in range(width // 128):
        c, s = coarse_cos[:, box : box + 1], coarse_sin[:, box : box + 1]
        cosines = c * fine_cos - s * fine_sin
        sines = s * fine_cos + c * fine_sin
        out_ref[0:GROUP, box * 128 : (box + 1) * 128] = cosines.astype(jnp.bfloat16)
        out_ref[GROUP : 2 * GROUP, box * 128 : (box + 1) * 128] = (-sines).astype(jnp.bfloat16)


def longitude_table(lower, blocks):
    width = NLON // lax.axis_size("lev")
    shifts, groups = np.array(blocks, np.int32).T
    return pl.pallas_call(
        table_kernel,
        grid_spec=pltpu.PrefetchScalarGridSpec(
            num_scalar_prefetch=3,
            grid=(len(blocks),),
            in_specs=[],
            out_specs=pl.BlockSpec((2 * GROUP, width), lambda i, *_: (i, 0)),
        ),
        out_shape=jax.ShapeDtypeStruct((len(blocks) * 2 * GROUP, width), jnp.bfloat16),
        compiler_params=pltpu.CompilerParams(vmem_limit_bytes=16 * MIB),
        cost_estimate=pl.CostEstimate(flops=1 << 10, bytes_accessed=1 << 10, transcendentals=0),
    )(jnp.asarray(shifts), jnp.asarray(groups), lower)


def longitude_kernel(layout, n_in, last, *refs):
    in_refs, table_ref, rest = refs[:n_in], refs[n_in], refs[n_in + 1 :]
    out_ref, left = rest[-2:]
    levs = lax.axis_size("lev")
    height = left.shape[0] // levs

    @pl.when(pl.program_id(0) == 0)
    def _():
        for shift, blocks in enumerate(layout):
            for place, (operand, group) in enumerate(blocks):
                left[shift * height : (shift + 1) * height, place * 2 * GROUP : (place + 1) * 2 * GROUP] = in_refs[
                    operand
                ][group]

    for shift in range(levs):
        here = slice(shift * height, (shift + 1) * height)
        values = jnp.dot(left[here], table_ref[...], preferred_element_type=jnp.float32)
        if len(rest) == 3:
            values = values + rest[0][here]
        if last:
            lev = lax.rem(lax.axis_index("lev") + levs - shift, levs)
            out_ref[lev] = values.reshape(out_ref.shape[1:]).astype(jnp.bfloat16)
        else:
            out_ref[here] = values


def longitude_part(pieces, table, total, last, columns):
    levs = len(pieces)
    height = pieces[0][0].shape[1]
    depth, width = table.shape
    tile = min(512, width)
    operands, layout = [], []
    for row in pieces:
        blocks = []
        for piece in row:
            blocks += [(len(operands), g) for g in range(piece.shape[0])]
            operands.append(piece)
        layout.append(blocks)
    n_in = len(operands)
    specs = [pl.BlockSpec(piece.shape, lambda j: (0, 0, 0)) for piece in operands]
    operands.append(table)
    specs.append(pl.BlockSpec((depth, tile), lambda j: (0, j)))
    if total is not None:
        operands.append(total)
        specs.append(pl.BlockSpec((levs * height, tile), lambda j: (0, j)))
    if last:
        out_spec = pl.BlockSpec((levs, columns, height // columns, tile), lambda j: (0, 0, 0, j))
        out_shape = jax.ShapeDtypeStruct((levs, columns, height // columns, width), jnp.bfloat16)
    else:
        out_spec = pl.BlockSpec((levs * height, tile), lambda j: (0, j))
        out_shape = jax.ShapeDtypeStruct((levs * height, width), jnp.float32)
    return pl.pallas_call(
        functools.partial(longitude_kernel, layout, n_in, last),
        grid=(width // tile,),
        in_specs=specs,
        out_specs=out_spec,
        out_shape=out_shape,
        scratch_shapes=[pltpu.VMEM((levs * height, depth), jnp.bfloat16)],
        compiler_params=pltpu.CompilerParams(vmem_limit_bytes=32 * MIB),
        cost_estimate=pl.CostEstimate(flops=1 << 10, bytes_accessed=1 << 10, transcendentals=0),
    )(*operands)


def send(array, axis, shift):
    size = lax.axis_size(axis)
    return lax.ppermute(array, axis, [(i, (i + shift) % size) for i in range(size)])


def shards(spectral, legendre, wave_order):
    slots, parts, columns, degrees = spectral.shape
    waves, levs = lax.axis_size("wave"), lax.axis_size("lev")
    rows, tiles = legendre.shape[1], degrees // 128
    groups = slots // GROUP
    spectral = spectral.reshape(slots, parts, columns, tiles, 128).transpose(0, 2, 3, 1, 4)
    legendre = legendre.reshape(slots, rows // 8, 8, tiles, 128).transpose(0, 1, 3, 2, 4)
    order, lower = pair_lists(wave_order, waves)
    sizes = list(CHUNKS) if groups == sum(CHUNKS) else [groups]
    far_first = sorted(range(1, waves), key=lambda shift: (abs(2 * shift - waves), shift))
    blocks, arrived = {}, {}
    first_group = 0
    lists = (order, lower)
    for chunk, size in enumerate(sizes):
        outs = legendre_part(spectral, legendre, lists, first_group, size)
        lists = lax.optimization_barrier((order, lower, outs[0]))[:2]
        for shift in [0] + far_first:
            piece = outs[shift]
            if shift != 0:
                if chunk > 0:
                    before = (chunk - 1, shift)
                    piece, arrived[before] = lax.optimization_barrier((piece, arrived[before]))
                piece = send(piece, "wave", shift)
            arrived[chunk, shift] = piece
            blocks[chunk, shift] = [(shift, first_group + g) for g in range(size)]
        first_group += size
    keys = list(arrived)
    late = []
    if len(sizes) > 1:
        late = [(len(sizes) - 1, shift) for shift in far_first]
    cut = [names for names in ([key for key in keys if key not in late], late) if names]
    pieces = {}

    def relay(key):
        before = (key[0] - 1, key[1])
        piece = arrived[key]
        if before in pieces:
            tied = lax.optimization_barrier((piece, *pieces[before]))
            piece, pieces[before] = tied[0], list(tied[1:])
        pieces[key] = [piece] + [send(piece, "lev", lev) for lev in range(1, levs)]

    final = [key for key in keys if key[0] == len(sizes) - 1 and key[1] != 0]
    for key in keys:
        if key not in final:
            relay(key)
    if len(sizes) > 1:
        first_relayed = (len(sizes) - 2, far_first[0])
        tied = lax.optimization_barrier((lists[1], *pieces[first_relayed]))
        lists, pieces[first_relayed] = (order, tied[0]), list(tied[1:])
    tables = [longitude_table(lists[1], [block for name in names for block in blocks[name]]) for names in cut]
    for key in final:
        tied = lax.optimization_barrier((arrived[key], *tables))
        arrived[key], tables = tied[0], list(tied[1:])
        relay(key)
    total = None
    for index, names in enumerate(cut):
        rows_of_pieces = [[pieces[name][lev] for name in names] for lev in range(levs)]
        total = longitude_part(rows_of_pieces, tables[index], total, index == len(cut) - 1, columns)
    return total


def solution(mesh):
    in_specs = (P(("member", "wave"), None, ("lev", "fld"), None), P("wave", None, None), P())
    out_specs = P(None, "fld", ("member", "wave"), "lev")
    return jax.shard_map(shards, mesh=mesh, in_specs=in_specs, out_specs=out_specs, check_vma=False)
```

```python
import functools
import math

import jax
import jax.numpy as jnp
import numpy as np
from jax import lax
from jax.experimental import pallas as pl
from jax.experimental.pallas import tpu as pltpu
from jax.sharding import PartitionSpec as P

NLON = 4096
PAIRS = 32
GROUP = 2 * PAIRS
STEP = 16
CHUNKS = (2, 2)
MIB = 1 << 20


def pair_lists(wave_order, waves):
    blocks = wave_order.reshape(waves, -1)
    slots = blocks.shape[1]
    rank = jnp.sum((blocks[:, None, :] < blocks[:, :, None]).astype(jnp.int32), axis=2)
    places = jnp.arange(slots, dtype=jnp.int32)
    hit = rank[:, None, :] == places[None, :, None]
    order = jnp.sum(jnp.where(hit, places[None, None, :], 0), axis=2)
    lower = jnp.sum(jnp.where(hit[:, : slots // 2], blocks[:, None, :], 0), axis=2)
    return order.reshape(-1), lower.reshape(-1)


def rows_of(values_ref, first, count):
    rows = lax.broadcasted_iota(jnp.int32, (8, 128), 0)
    pieces = []
    for base in range(0, count, 8):
        piece = jnp.full((8, 128), values_ref[first + base], jnp.int32)
        for row in range(1, 8):
            piece = jnp.where(rows == row, values_ref[first + base + row], piece)
        pieces.append(piece)
    return jnp.concatenate(pieces, axis=0)


def legendre_kernel(first_group, groups, order_ref, lower_ref, spectral_ref, legendre_ref, *rest):
    waves = lax.axis_size("wave")
    out_refs = rest[:waves]
    coeffs_ref, values_ref, by_slot, turned, sems = rest[waves:]
    columns, tiles = spectral_ref.shape[1], spectral_ref.shape[2]
    rows = 8 * legendre_ref.shape[1]
    mine = lax.axis_index("wave")
    slots_here = spectral_ref.shape[0]
    group = pl.program_id(0)
    steps = PAIRS // STEP

    @pl.when(group == 0)
    def _():
        @pl.loop(0, groups * PAIRS, unroll=4)
        def _(p):
            rank = first_group * PAIRS + p
            low = order_ref[mine * slots_here + rank]
            high = order_ref[mine * slots_here + slots_here - 1 - rank]
            t = lower_ref[mine * (slots_here // 2) + rank] // 128
            for kind, (source, target) in enumerate(((legendre_ref, values_ref), (spectral_ref, coeffs_ref))):
                sem = sems.at[kind, p // STEP]
                pltpu.make_async_copy(
                    source.at[low, :, pl.ds(t, tiles - t)], target.at[p, :, pl.ds(0, tiles - t)], sem
                ).start()
                pltpu.make_async_copy(
                    source.at[high, :, pl.ds(tiles - 1 - t, t + 1)], target.at[p, :, pl.ds(tiles - t, t + 1)], sem
                ).start()

    lanes = lax.broadcasted_iota(jnp.int32, (STEP, 128), 1)

    @pl.loop(0, steps)
    def _(step):
        place = group * steps + step
        first = place * STEP
        wavenums = rows_of(lower_ref, mine * (slots_here // 2) + first_group * PAIRS + first, STEP)
        for kind, target in enumerate((values_ref, coeffs_ref)):
            arrived = target.at[pl.ds(first, STEP)]
            pltpu.make_async_copy(arrived, arrived, sems.at[kind, place]).wait()
        t, inside = wavenums // 128, wavenums & 127
        parity = jnp.where(((lanes + wavenums) & 1) == 1, -1.0, 1.0)
        always = tiles // 2 + 1
        low_keep, low_sign, high_keep, high_sign = [], [], [], []
        for i in range(tiles + 1):
            if i == 0:
                low = jnp.where(lanes >= inside, 1.0, 0.0)
            else:
                low = jnp.where(t + i < tiles, 1.0, 0.0)
            high = jnp.where((t + i > tiles) | ((t + i == tiles) & (lanes >= 127 - inside)), 1.0, 0.0)
            if i < tiles:
                low_keep.append(low.astype(jnp.bfloat16))
                low_sign.append((low * parity).astype(jnp.bfloat16))
            if i >= always:
                high_keep.append(high.astype(jnp.bfloat16))
                high_sign.append((-high * parity).astype(jnp.bfloat16))
        low_keep, low_sign, high_keep, high_sign = [
            jnp.concatenate(mask, axis=1) for mask in (low_keep, low_sign, high_keep, high_sign)
        ]
        for s in range(STEP):
            row = slice(s, s + 1)
            coeffs = jnp.concatenate(
                [coeffs_ref[first + s, :, i].reshape(2 * columns, 128) for i in range(tiles + 1)], axis=1
            )
            values = jnp.concatenate([values_ref[first + s, :, i].reshape(rows, 128) for i in range(tiles + 1)], axis=1)
            for place, part, keep, sign in (
                (step * STEP + s, slice(0, tiles * 128), low_keep, low_sign),
                (PAIRS + step * STEP + s, slice(always * 128, (tiles + 1) * 128), high_keep, high_sign),
            ):
                left = jnp.concatenate([coeffs[:, part] * keep[row], coeffs[:, part] * sign[row]], axis=0)
                by_slot[:, place, :] = lax.dot_general(
                    left, values[:, part], (((1,), (1,)), ((), ())), preferred_element_type=jnp.float32
                )

    for pair in range(2 * columns):
        both = jnp.concatenate([by_slot[2 * pair], by_slot[2 * pair + 1]], axis=0)
        turned[pair] = both.astype(jnp.bfloat16).T.astype(turned.dtype)
    rows_dest = 2 * rows // waves
    half = waves // 2
    for shift in range(waves):
        dest = lax.rem(mine + shift, waves)
        side, block = dest // half, lax.rem(dest, half)
        piece = turned[
            pl.ds(side * columns, columns), pl.ds(pl.multiple_of(block * rows_dest, rows_dest), rows_dest), :
        ]
        out_refs[shift][0] = piece.reshape(columns * rows_dest, 2 * GROUP).astype(jnp.bfloat16)


def legendre_part(spectral, legendre, lists, first_group, groups):
    waves = lax.axis_size("wave")
    slots, columns, tiles = spectral.shape[:3]
    rows = 8 * legendre.shape[1]
    rows_dest = 2 * rows // waves
    pairs = groups * PAIRS
    shape = jax.ShapeDtypeStruct((groups, columns * rows_dest, 2 * GROUP), jnp.bfloat16)
    return pl.pallas_call(
        functools.partial(legendre_kernel, first_group, groups),
        grid_spec=pltpu.PrefetchScalarGridSpec(
            num_scalar_prefetch=2,
            grid=(groups,),
            in_specs=[pl.BlockSpec(memory_space=pl.ANY)] * 2,
            out_specs=[pl.BlockSpec((1,) + shape.shape[1:], lambda g, *_: (g, 0, 0))] * waves,
            scratch_shapes=[
                pltpu.VMEM((pairs, columns, tiles + 1, 2, 128), jnp.bfloat16),
                pltpu.VMEM((pairs, rows // 8, tiles + 1, 8, 128), jnp.bfloat16),
                pltpu.VMEM((4 * columns, GROUP, rows), jnp.float32),
                pltpu.VMEM((2 * columns, rows, 2 * GROUP), jnp.float32),
                pltpu.SemaphoreType.DMA((2, pairs // STEP)),
            ],
        ),
        out_shape=[shape] * waves,
        compiler_params=pltpu.CompilerParams(vmem_limit_bytes=56 * MIB),
        cost_estimate=pl.CostEstimate(flops=1 << 10, bytes_accessed=1 << 10, transcendentals=0),
    )(*lists, spectral, legendre)


def cos_sin(phase):
    quarter = NLON // 4
    quadrant = (phase + quarter // 2) // quarter
    x = (phase - quadrant * quarter).astype(jnp.float32) * (2.0 * math.pi / NLON)
    y = x * x
    sine = x * (1.0 + y * (-1.0 / 6 + y * (1.0 / 120 + y * (-1.0 / 5040 + y * (1.0 / 362880)))))
    cosine = 1.0 + y * (-0.5 + y * (1.0 / 24 + y * (-1.0 / 720 + y * (1.0 / 40320 + y * (-1.0 / 3628800)))))
    swap = (quadrant & 1) == 1
    c = jnp.where(swap, sine, cosine)
    s = jnp.where(swap, cosine, sine)
    c = jnp.where(((quadrant + 1) & 2) == 2, -c, c)
    s = jnp.where((quadrant & 2) == 2, -s, s)
    return c, s


def table_kernel(per_step, shifts_ref, groups_ref, lower_ref, out_ref):
    waves = lax.axis_size("wave")
    pairs_here = lower_ref.shape[0] // waves
    width = out_ref.shape[1]
    lon_start = lax.axis_index("lev") * width
    lanes = lax.broadcasted_iota(jnp.int32, (GROUP, 128), 1)
    for k in range(per_step):
        place = pl.program_id(0) * per_step + k
        source = lax.rem(lax.axis_index("wave") + waves - shifts_ref[place], waves)
        lower = rows_of(lower_ref, source * pairs_here + groups_ref[place] * PAIRS, PAIRS)
        wavenums = jnp.concatenate([lower, 2 * lower_ref.shape[0] - 1 - lower], axis=0)
        fine_cos, fine_sin = cos_sin((wavenums * lanes) & (NLON - 1))
        coarse_cos, coarse_sin = cos_sin((wavenums * (lon_start + 128 * lanes)) & (NLON - 1))
        weight = jnp.where(wavenums == 0, 1.0, 2.0)
        coarse_cos, coarse_sin = coarse_cos * weight, coarse_sin * weight
        first, second = slice(2 * k * GROUP, (2 * k + 1) * GROUP), slice((2 * k + 1) * GROUP, (2 * k + 2) * GROUP)
        for box in range(width // 128):
            c, s = coarse_cos[:, box : box + 1], coarse_sin[:, box : box + 1]
            cosines = c * fine_cos - s * fine_sin
            sines = s * fine_cos + c * fine_sin
            out_ref[first, box * 128 : (box + 1) * 128] = cosines.astype(jnp.bfloat16)
            out_ref[second, box * 128 : (box + 1) * 128] = (-sines).astype(jnp.bfloat16)


def longitude_table(lower, blocks):
    width = NLON // lax.axis_size("lev")
    per_step = 2 - len(blocks) % 2
    shifts, groups = np.array(blocks, np.int32).T
    return pl.pallas_call(
        functools.partial(table_kernel, per_step),
        grid_spec=pltpu.PrefetchScalarGridSpec(
            num_scalar_prefetch=3,
            grid=(len(blocks) // per_step,),
            in_specs=[],
            out_specs=pl.BlockSpec((per_step * 2 * GROUP, width), lambda i, *_: (i, 0)),
        ),
        out_shape=jax.ShapeDtypeStruct((len(blocks) * 2 * GROUP, width), jnp.bfloat16),
        compiler_params=pltpu.CompilerParams(vmem_limit_bytes=16 * MIB),
        cost_estimate=pl.CostEstimate(flops=1 << 10, bytes_accessed=1 << 10, transcendentals=0),
    )(jnp.asarray(shifts), jnp.asarray(groups), lower)


def longitude_kernel(layout, n_in, last, *refs):
    in_refs, table_ref, rest = refs[:n_in], refs[n_in], refs[n_in + 1 :]
    out_ref, left = rest[-2:]
    levs = lax.axis_size("lev")
    height = left.shape[0] // levs

    @pl.when(pl.program_id(0) == 0)
    def _():
        for shift, blocks in enumerate(layout):
            for place, (operand, group) in enumerate(blocks):
                left[shift * height : (shift + 1) * height, place * 2 * GROUP : (place + 1) * 2 * GROUP] = in_refs[
                    operand
                ][group]

    for shift in range(levs):
        here = slice(shift * height, (shift + 1) * height)
        values = jnp.dot(left[here], table_ref[...], preferred_element_type=jnp.float32)
        if len(rest) == 3:
            values = values + rest[0][here]
        if last:
            lev = lax.rem(lax.axis_index("lev") + levs - shift, levs)
            out_ref[lev] = values.reshape(out_ref.shape[1:]).astype(jnp.bfloat16)
        else:
            out_ref[here] = values


def longitude_part(pieces, table, total, last, columns):
    levs = len(pieces)
    height = pieces[0][0].shape[1]
    depth, width = table.shape
    tile = min(1024 if last else 512, width)
    operands, layout = [], []
    for row in pieces:
        blocks = []
        for piece in row:
            blocks += [(len(operands), g) for g in range(piece.shape[0])]
            operands.append(piece)
        layout.append(blocks)
    n_in = len(operands)
    specs = [pl.BlockSpec(piece.shape, lambda j: (0, 0, 0)) for piece in operands]
    operands.append(table)
    specs.append(pl.BlockSpec((depth, tile), lambda j: (0, j)))
    if total is not None:
        operands.append(total)
        specs.append(pl.BlockSpec((levs * height, tile), lambda j: (0, j)))
    if last:
        out_spec = pl.BlockSpec((levs, columns, height // columns, tile), lambda j: (0, 0, 0, j))
        out_shape = jax.ShapeDtypeStruct((levs, columns, height // columns, width), jnp.bfloat16)
    else:
        out_spec = pl.BlockSpec((levs * height, tile), lambda j: (0, j))
        out_shape = jax.ShapeDtypeStruct((levs * height, width), jnp.float32)
    return pl.pallas_call(
        functools.partial(longitude_kernel, layout, n_in, last),
        grid=(width // tile,),
        in_specs=specs,
        out_specs=out_spec,
        out_shape=out_shape,
        scratch_shapes=[pltpu.VMEM((levs * height, depth), jnp.bfloat16)],
        compiler_params=pltpu.CompilerParams(vmem_limit_bytes=32 * MIB),
        cost_estimate=pl.CostEstimate(flops=1 << 10, bytes_accessed=1 << 10, transcendentals=0),
    )(*operands)


def send(array, axis, shift):
    size = lax.axis_size(axis)
    return lax.ppermute(array, axis, [(i, (i + shift) % size) for i in range(size)])


def shards(spectral, legendre, wave_order):
    slots, parts, columns, degrees = spectral.shape
    waves, levs = lax.axis_size("wave"), lax.axis_size("lev")
    rows, tiles = legendre.shape[1], degrees // 128
    groups = slots // GROUP
    spectral = spectral.reshape(slots, parts, columns, tiles, 128).transpose(0, 2, 3, 1, 4)
    legendre = legendre.reshape(slots, rows // 8, 8, tiles, 128).transpose(0, 1, 3, 2, 4)
    order, lower = pair_lists(wave_order, waves)
    sizes = list(CHUNKS) if groups == sum(CHUNKS) else [groups]
    far_first = sorted(range(1, waves), key=lambda shift: (abs(2 * shift - waves), shift))
    blocks, arrived = {}, {}
    first_group = 0
    lists = (order, lower)
    for chunk, size in enumerate(sizes):
        outs = legendre_part(spectral, legendre, lists, first_group, size)
        lists = lax.optimization_barrier((order, lower, outs[0]))[:2]
        for shift in [0] + far_first:
            piece = outs[shift]
            if shift != 0:
                if chunk > 0:
                    before = (chunk - 1, shift)
                    piece, arrived[before] = lax.optimization_barrier((piece, arrived[before]))
                piece = send(piece, "wave", shift)
            arrived[chunk, shift] = piece
            blocks[chunk, shift] = [(shift, first_group + g) for g in range(size)]
        first_group += size
    keys = list(arrived)
    late = []
    if len(sizes) > 1:
        late = [(len(sizes) - 1, shift) for shift in far_first[1:]]
    cut = [names for names in ([key for key in keys if key not in late], late) if names]
    pieces = {}

    def relay(key):
        before = (key[0] - 1, key[1])
        piece = arrived[key]
        if before in pieces:
            tied = lax.optimization_barrier((piece, *pieces[before]))
            piece, pieces[before] = tied[0], list(tied[1:])
        pieces[key] = [piece] + [send(piece, "lev", lev) for lev in range(1, levs)]

    final = [key for key in keys if key[0] == len(sizes) - 1 and key[1] != 0]
    for key in keys:
        if key not in final:
            relay(key)
    if len(sizes) > 1:
        early = [(len(sizes) - 2, far_first[0]), (len(sizes) - 1, 0)]
        tied = lax.optimization_barrier((lists[1], [pieces[key] for key in early]))
        lists = (order, tied[0])
        pieces.update(zip(early, tied[1]))
    tables = [longitude_table(lists[1], [block for name in names for block in blocks[name]]) for names in cut]
    for key in final:
        count = 2 if key == final[-1] else 1
        held = lax.optimization_barrier((arrived[key], tables[:count]))
        arrived[key], tables[:count] = held
        relay(key)
    total = None
    for index, names in enumerate(cut):
        rows_of_pieces = [[pieces[name][lev] for name in names] for lev in range(levs)]
        total = longitude_part(rows_of_pieces, tables[index], total, index == len(cut) - 1, columns)
    return total


def solution(mesh):
    in_specs = (P(("member", "wave"), None, ("lev", "fld"), None), P("wave", None, None), P())
    out_specs = P(None, "fld", ("member", "wave"), "lev")
    return jax.shard_map(shards, mesh=mesh, in_specs=in_specs, out_specs=out_specs, check_vma=False)
```

```python
import functools
import math

import jax
import jax.numpy as jnp
import numpy as np
from jax import lax
from jax.experimental import pallas as pl
from jax.experimental.pallas import tpu as pltpu
from jax.sharding import PartitionSpec as P

NLON = 4096
PAIRS = 32
GROUP = 2 * PAIRS
STEP = 16
CHUNKS = (2, 2)
MIB = 1 << 20


def pair_lists(wave_order, waves):
    blocks = wave_order.reshape(waves, -1)
    slots = blocks.shape[1]
    rank = jnp.sum((blocks[:, None, :] < blocks[:, :, None]).astype(jnp.int32), axis=2)
    places = jnp.arange(slots, dtype=jnp.int32)
    hit = rank[:, None, :] == places[None, :, None]
    order = jnp.sum(jnp.where(hit, places[None, None, :], 0), axis=2)
    lower = jnp.sum(jnp.where(hit[:, : slots // 2], blocks[:, None, :], 0), axis=2)
    return order.reshape(-1), lower.reshape(-1)


def rows_of(values_ref, first, count):
    rows = lax.broadcasted_iota(jnp.int32, (8, 128), 0)
    pieces = []
    for base in range(0, count, 8):
        piece = jnp.full((8, 128), values_ref[first + base], jnp.int32)
        for row in range(1, 8):
            piece = jnp.where(rows == row, values_ref[first + base + row], piece)
        pieces.append(piece)
    return jnp.concatenate(pieces, axis=0)


def legendre_kernel(first_group, groups, order_ref, lower_ref, spectral_ref, legendre_ref, *rest):
    waves = lax.axis_size("wave")
    out_refs = rest[:waves]
    coeffs_ref, values_ref, by_slot, turned, sems = rest[waves:]
    columns, tiles = spectral_ref.shape[1], spectral_ref.shape[2]
    rows = legendre_ref.shape[1]
    mine = lax.axis_index("wave")
    slots_here = spectral_ref.shape[0]
    group = pl.program_id(0)
    steps = PAIRS // STEP

    @pl.when(group == 0)
    def _():
        @pl.loop(0, groups * PAIRS, unroll=4)
        def _(p):
            rank = first_group * PAIRS + p
            low = order_ref[mine * slots_here + rank]
            high = order_ref[mine * slots_here + slots_here - 1 - rank]
            t = lower_ref[mine * (slots_here // 2) + rank] // 128
            sem = sems.at[1, p // STEP]
            pltpu.make_async_copy(
                spectral_ref.at[low, :, pl.ds(t, tiles - t)], coeffs_ref.at[p, :, pl.ds(0, tiles - t)], sem
            ).start()
            pltpu.make_async_copy(
                spectral_ref.at[high, :, pl.ds(tiles - 1 - t, t + 1)], coeffs_ref.at[p, :, pl.ds(tiles - t, t + 1)], sem
            ).start()
            for first in range(tiles // 2):

                @pl.when(t == first)
                def _(first=first):
                    split, end = (tiles - first) * 128, (tiles + 1) * 128
                    pltpu.make_async_copy(
                        legendre_ref.at[low, :, first * 128 : tiles * 128],
                        values_ref.at[p, :, 0:split],
                        sems.at[0, p // STEP],
                    ).start()
                    pltpu.make_async_copy(
                        legendre_ref.at[high, :, (tiles - 1 - first) * 128 : tiles * 128],
                        values_ref.at[p, :, split:end],
                        sems.at[0, p // STEP],
                    ).start()

    lanes = lax.broadcasted_iota(jnp.int32, (STEP, 128), 1)

    @pl.loop(0, steps)
    def _(step):
        place = group * steps + step
        first = place * STEP
        wavenums = rows_of(lower_ref, mine * (slots_here // 2) + first_group * PAIRS + first, STEP)
        for kind, target in enumerate((values_ref, coeffs_ref)):
            arrived = target.at[pl.ds(first, STEP)]
            pltpu.make_async_copy(arrived, arrived, sems.at[kind, place]).wait()
        t, inside = wavenums // 128, wavenums & 127
        parity = jnp.where(((lanes + wavenums) & 1) == 1, -1.0, 1.0)
        always = tiles // 2 + 1
        low_keep, low_sign, high_keep, high_sign = [], [], [], []
        for i in range(tiles + 1):
            if i == 0:
                low = jnp.where(lanes >= inside, 1.0, 0.0)
            else:
                low = jnp.where(t + i < tiles, 1.0, 0.0)
            high = jnp.where((t + i > tiles) | ((t + i == tiles) & (lanes >= 127 - inside)), 1.0, 0.0)
            if i < tiles:
                low_keep.append(low.astype(jnp.bfloat16))
                low_sign.append((low * parity).astype(jnp.bfloat16))
            if i >= always:
                high_keep.append(high.astype(jnp.bfloat16))
                high_sign.append((-high * parity).astype(jnp.bfloat16))
        low_keep, low_sign, high_keep, high_sign = [
            jnp.concatenate(mask, axis=1) for mask in (low_keep, low_sign, high_keep, high_sign)
        ]
        for s in range(STEP):
            row = slice(s, s + 1)
            coeffs = jnp.concatenate(
                [coeffs_ref[first + s, :, i].reshape(2 * columns, 128) for i in range(tiles + 1)], axis=1
            )
            values = values_ref[first + s]
            for place, part, keep, sign in (
                (step * STEP + s, slice(0, tiles * 128), low_keep, low_sign),
                (PAIRS + step * STEP + s, slice(always * 128, (tiles + 1) * 128), high_keep, high_sign),
            ):
                left = jnp.concatenate([coeffs[:, part] * keep[row], coeffs[:, part] * sign[row]], axis=0)
                by_slot[:, place, :] = lax.dot_general(
                    left, values[:, part], (((1,), (1,)), ((), ())), preferred_element_type=jnp.float32
                )

    for pair in range(2 * columns):
        both = jnp.concatenate([by_slot[2 * pair], by_slot[2 * pair + 1]], axis=0)
        turned[pair] = both.astype(jnp.bfloat16).T.astype(turned.dtype)
    rows_dest = 2 * rows // waves
    half = waves // 2
    for shift in range(waves):
        dest = lax.rem(mine + shift, waves)
        side, block = dest // half, lax.rem(dest, half)
        piece = turned[
            pl.ds(side * columns, columns), pl.ds(pl.multiple_of(block * rows_dest, rows_dest), rows_dest), :
        ]
        out_refs[shift][0] = piece.reshape(columns * rows_dest, 2 * GROUP).astype(jnp.bfloat16)


def legendre_part(spectral, legendre, lists, first_group, groups):
    waves = lax.axis_size("wave")
    slots, columns, tiles = spectral.shape[:3]
    rows = legendre.shape[1]
    rows_dest = 2 * rows // waves
    pairs = groups * PAIRS
    shape = jax.ShapeDtypeStruct((groups, columns * rows_dest, 2 * GROUP), jnp.bfloat16)
    return pl.pallas_call(
        functools.partial(legendre_kernel, first_group, groups),
        grid_spec=pltpu.PrefetchScalarGridSpec(
            num_scalar_prefetch=2,
            grid=(groups,),
            in_specs=[pl.BlockSpec(memory_space=pl.ANY)] * 2,
            out_specs=[pl.BlockSpec((1,) + shape.shape[1:], lambda g, *_: (g, 0, 0))] * waves,
            scratch_shapes=[
                pltpu.VMEM((pairs, columns, tiles + 1, 2, 128), jnp.bfloat16),
                pltpu.VMEM((pairs, rows, (tiles + 1) * 128), jnp.bfloat16),
                pltpu.VMEM((4 * columns, GROUP, rows), jnp.float32),
                pltpu.VMEM((2 * columns, rows, 2 * GROUP), jnp.float32),
                pltpu.SemaphoreType.DMA((2, pairs // STEP)),
            ],
        ),
        out_shape=[shape] * waves,
        compiler_params=pltpu.CompilerParams(vmem_limit_bytes=56 * MIB),
        cost_estimate=pl.CostEstimate(flops=1 << 10, bytes_accessed=1 << 10, transcendentals=0),
    )(*lists, spectral, legendre)


def cos_sin(phase):
    quarter = NLON // 4
    quadrant = (phase + quarter // 2) // quarter
    x = (phase - quadrant * quarter).astype(jnp.float32) * (2.0 * math.pi / NLON)
    y = x * x
    sine = x * (1.0 + y * (-1.0 / 6 + y * (1.0 / 120 + y * (-1.0 / 5040 + y * (1.0 / 362880)))))
    cosine = 1.0 + y * (-0.5 + y * (1.0 / 24 + y * (-1.0 / 720 + y * (1.0 / 40320 + y * (-1.0 / 3628800)))))
    swap = (quadrant & 1) == 1
    c = jnp.where(swap, sine, cosine)
    s = jnp.where(swap, cosine, sine)
    c = jnp.where(((quadrant + 1) & 2) == 2, -c, c)
    s = jnp.where((quadrant & 2) == 2, -s, s)
    return c, s


def table_kernel(per_step, shifts_ref, groups_ref, lower_ref, out_ref):
    waves = lax.axis_size("wave")
    pairs_here = lower_ref.shape[0] // waves
    width = out_ref.shape[1]
    lon_start = lax.axis_index("lev") * width
    lanes = lax.broadcasted_iota(jnp.int32, (GROUP, 128), 1)
    for k in range(per_step):
        place = pl.program_id(0) * per_step + k
        source = lax.rem(lax.axis_index("wave") + waves - shifts_ref[place], waves)
        lower = rows_of(lower_ref, source * pairs_here + groups_ref[place] * PAIRS, PAIRS)
        wavenums = jnp.concatenate([lower, 2 * lower_ref.shape[0] - 1 - lower], axis=0)
        fine_cos, fine_sin = cos_sin((wavenums * lanes) & (NLON - 1))
        coarse_cos, coarse_sin = cos_sin((wavenums * (lon_start + 128 * lanes)) & (NLON - 1))
        weight = jnp.where(wavenums == 0, 1.0, 2.0)
        coarse_cos, coarse_sin = coarse_cos * weight, coarse_sin * weight
        first, second = slice(2 * k * GROUP, (2 * k + 1) * GROUP), slice((2 * k + 1) * GROUP, (2 * k + 2) * GROUP)
        for box in range(width // 128):
            c, s = coarse_cos[:, box : box + 1], coarse_sin[:, box : box + 1]
            cosines = c * fine_cos - s * fine_sin
            sines = s * fine_cos + c * fine_sin
            out_ref[first, box * 128 : (box + 1) * 128] = cosines.astype(jnp.bfloat16)
            out_ref[second, box * 128 : (box + 1) * 128] = (-sines).astype(jnp.bfloat16)


def longitude_table(lower, blocks):
    width = NLON // lax.axis_size("lev")
    per_step = 2 - len(blocks) % 2
    shifts, groups = np.array(blocks, np.int32).T
    return pl.pallas_call(
        functools.partial(table_kernel, per_step),
        grid_spec=pltpu.PrefetchScalarGridSpec(
            num_scalar_prefetch=3,
            grid=(len(blocks) // per_step,),
            in_specs=[],
            out_specs=pl.BlockSpec((per_step * 2 * GROUP, width), lambda i, *_: (i, 0)),
        ),
        out_shape=jax.ShapeDtypeStruct((len(blocks) * 2 * GROUP, width), jnp.bfloat16),
        compiler_params=pltpu.CompilerParams(vmem_limit_bytes=16 * MIB),
        cost_estimate=pl.CostEstimate(flops=1 << 10, bytes_accessed=1 << 10, transcendentals=0),
    )(jnp.asarray(shifts), jnp.asarray(groups), lower)


def longitude_kernel(layout, n_in, last, *refs):
    in_refs, table_ref, rest = refs[:n_in], refs[n_in], refs[n_in + 1 :]
    out_ref, left = rest[-2:]
    levs = lax.axis_size("lev")
    height = left.shape[0] // levs

    @pl.when(pl.program_id(0) == 0)
    def _():
        for shift, blocks in enumerate(layout):
            for place, (operand, group) in enumerate(blocks):
                left[shift * height : (shift + 1) * height, place * 2 * GROUP : (place + 1) * 2 * GROUP] = in_refs[
                    operand
                ][group]

    for shift in range(levs):
        here = slice(shift * height, (shift + 1) * height)
        values = jnp.dot(left[here], table_ref[...], preferred_element_type=jnp.float32)
        if len(rest) == 3:
            values = values + rest[0][here]
        if last:
            lev = lax.rem(lax.axis_index("lev") + levs - shift, levs)
            out_ref[lev] = values.reshape(out_ref.shape[1:]).astype(jnp.bfloat16)
        else:
            out_ref[here] = values


def longitude_part(pieces, table, total, last, columns):
    levs = len(pieces)
    height = pieces[0][0].shape[1]
    depth, width = table.shape
    tile = min(1024 if last else 512, width)
    operands, layout = [], []
    for row in pieces:
        blocks = []
        for piece in row:
            blocks += [(len(operands), g) for g in range(piece.shape[0])]
            operands.append(piece)
        layout.append(blocks)
    n_in = len(operands)
    specs = [pl.BlockSpec(piece.shape, lambda j: (0, 0, 0)) for piece in operands]
    operands.append(table)
    specs.append(pl.BlockSpec((depth, tile), lambda j: (0, j)))
    if total is not None:
        operands.append(total)
        specs.append(pl.BlockSpec((levs * height, tile), lambda j: (0, j)))
    if last:
        out_spec = pl.BlockSpec((levs, columns, height // columns, tile), lambda j: (0, 0, 0, j))
        out_shape = jax.ShapeDtypeStruct((levs, columns, height // columns, width), jnp.bfloat16)
    else:
        out_spec = pl.BlockSpec((levs * height, tile), lambda j: (0, j))
        out_shape = jax.ShapeDtypeStruct((levs * height, width), jnp.float32)
    return pl.pallas_call(
        functools.partial(longitude_kernel, layout, n_in, last),
        grid=(width // tile,),
        in_specs=specs,
        out_specs=out_spec,
        out_shape=out_shape,
        scratch_shapes=[pltpu.VMEM((levs * height, depth), jnp.bfloat16)],
        compiler_params=pltpu.CompilerParams(vmem_limit_bytes=32 * MIB),
        cost_estimate=pl.CostEstimate(flops=1 << 10, bytes_accessed=1 << 10, transcendentals=0),
    )(*operands)


def send(array, axis, shift):
    size = lax.axis_size(axis)
    return lax.ppermute(array, axis, [(i, (i + shift) % size) for i in range(size)])


def shards(spectral, legendre, wave_order):
    slots, parts, columns, degrees = spectral.shape
    waves, levs = lax.axis_size("wave"), lax.axis_size("lev")
    tiles = degrees // 128
    groups = slots // GROUP
    spectral = spectral.reshape(slots, parts, columns, tiles, 128).transpose(0, 2, 3, 1, 4)
    order, lower = pair_lists(wave_order, waves)
    sizes = list(CHUNKS) if groups == sum(CHUNKS) else [groups]
    far_first = sorted(range(1, waves), key=lambda shift: (abs(2 * shift - waves), shift))
    blocks, arrived = {}, {}
    first_group = 0
    lists = (order, lower)
    for chunk, size in enumerate(sizes):
        outs = legendre_part(spectral, legendre, lists, first_group, size)
        lists = lax.optimization_barrier((order, lower, outs[0]))[:2]
        for shift in [0] + far_first:
            piece = outs[shift]
            if shift != 0:
                if chunk > 0:
                    before = (chunk - 1, shift)
                    piece, arrived[before] = lax.optimization_barrier((piece, arrived[before]))
                piece = send(piece, "wave", shift)
            arrived[chunk, shift] = piece
            blocks[chunk, shift] = [(shift, first_group + g) for g in range(size)]
        first_group += size
    keys = list(arrived)
    late = []
    if len(sizes) > 1:
        late = [(len(sizes) - 1, shift) for shift in far_first[1:]]
    cut = [names for names in ([key for key in keys if key not in late], late) if names]
    pieces = {}

    def relay(key):
        before = (key[0] - 1, key[1])
        piece = arrived[key]
        if before in pieces:
            tied = lax.optimization_barrier((piece, *pieces[before]))
            piece, pieces[before] = tied[0], list(tied[1:])
        pieces[key] = [piece] + [send(piece, "lev", lev) for lev in range(1, levs)]

    final = [key for key in keys if key[0] == len(sizes) - 1 and key[1] != 0]
    for key in keys:
        if key not in final:
            relay(key)
    if len(sizes) > 1:
        early = [(len(sizes) - 2, far_first[0]), (len(sizes) - 1, 0)]
        tied = lax.optimization_barrier((lists[1], [pieces[key] for key in early]))
        lists = (order, tied[0])
        pieces.update(zip(early, tied[1]))
    tables = [longitude_table(lists[1], [block for name in names for block in blocks[name]]) for names in cut]
    for key in final:
        count = 2 if key == final[-1] else 1
        held = lax.optimization_barrier((arrived[key], tables[:count]))
        arrived[key], tables[:count] = held
        relay(key)
    total = None
    for index, names in enumerate(cut):
        rows_of_pieces = [[pieces[name][lev] for name in names] for lev in range(levs)]
        total = longitude_part(rows_of_pieces, tables[index], total, index == len(cut) - 1, columns)
    return total


def solution(mesh):
    in_specs = (P(("member", "wave"), None, ("lev", "fld"), None), P("wave", None, None), P())
    out_specs = P(None, "fld", ("member", "wave"), "lev")
    return jax.shard_map(shards, mesh=mesh, in_specs=in_specs, out_specs=out_specs, check_vma=False)
```
